256 devices in a mesh: atoms: 16 (over x, y), energy: 16 (over z, core).
Axes of the slice: x: 4, y: 4, z: 8, core: 2. Of those that a mesh axis runs over, the one named last changes fastest.
Arguments:
- retarded_green_blocks: bfloat16 [16, 48, 2, 384, 384], P('atoms', 'energy'), may hold values from -0.21875 to 0.21875
- contact_lesser_sigma: bfloat16 [16, 48, 2, 384, 384], P('atoms', 'energy'), may hold values from -6 to 6
- energy_counts: int32 [16], replicated, may hold values from 1 to 3, 30 in all
- phonon_shift: int32 [64], replicated, may hold values from 1 to 15
- phonon_weight: float32 [4, 64], replicated, may hold values from 0.01 to 0.1
Outputs:
- scattered: bfloat16 [16, 48, 2, 384, 384], P('atoms', 'energy')
The draws below stay inside these ranges and needn't reach their ends.
Inputs may be any that keep to these rules, and one draw needn't show every extreme that they name: energy_counts sums to 30; its largest entry is exactly 3.
All inputs are finite; a program needn't handle non-finite values.
Results may differ from the reference program's by a relative error of at most 0.007.
Values may be sent and summed in bfloat16 or wider, within the bound.
No kernel may reach another device: no remote copies, remote signals or barrier semaphores. Data moves between devices by JAX's collectives and lax.ppermute only.
A program may use at most 64 MiB of HBM per device.

```python
import math
import jax
import jax.numpy as jnp
import numpy as np
from jax import lax

BLOCK_ORBITALS = 384
NW = 64
NE_DEV = 3
ENERGY_SLOTS = 48
TOTAL = 30
SLAB_BLOCKS = 16
N_ENERGY = 16


def place_ends(values, stream_key, smallest, largest):
    longest = values.shape.index(max(values.shape))
    spots = []
    for shift in (0, 1):
        where = [jax.random.randint(jax.random.fold_in(stream_key, axis), (), 0, length) for axis, length in enumerate(values.shape)]
        where[longest] = (where[longest] + shift) % values.shape[longest]
        spots.append(tuple(where))
    return values.at[spots[0]].set(smallest).at[spots[1]].set(largest)


def levels(stream_key, shape, split, least, top_value):
    factor_of, own = 1.0, jax.random.fold_in(stream_key, 6)
    for position, shards_of in split:
        draws = jnp.exp(jax.random.uniform(jax.random.fold_in(own, position), (shards_of,), jnp.float32, least / len(split), top_value / len(split)))
        factor_of = factor_of * jnp.repeat(draws, shape[position] // shards_of).reshape([-1 if axis == position else 1 for axis in range(len(shape))])
    return factor_of


def profile(amount, total, most, lean):
    loads = [(1 << 20) // math.isqrt(standing ** lean) + 1 for standing in range(2, amount + 1)]
    spare, given = total - most - (amount - 1), [1] * (amount - 1)
    while spare > 0:
        candidates = [i for i in range(amount - 1) if given[i] < most]
        whole, remaining = sum([loads[i] for i in candidates]), spare
        for i in candidates:
            more = min(most - given[i], max(1, remaining * loads[i] // whole), spare)
            given[i] = given[i] + more
            spare = spare - more
    return np.array([most] + given)


def uneven_parts(key, number_of, total, bound, skew):
    if number_of == 2:
        one = jax.random.randint(key, (), max(1, total - bound), min(bound, total - 1) + 1)
        return jnp.stack([one, total - one])
    sizes = jnp.asarray(profile(number_of, total, bound, skew), jnp.int32)
    pairs = (number_of - 1) // 2
    source_of, taker = sizes[1:1 + 2 * pairs:2], sizes[2:2 + 2 * pairs:2]
    slack = jnp.minimum(source_of - 1, bound - taker)
    shifted = jax.random.randint(jax.random.fold_in(key, 1), (pairs,), 0, 1 << 20) % (slack + 1)
    sizes = sizes.at[1:1 + 2 * pairs:2].set(source_of - shifted).at[2:2 + 2 * pairs:2].set(taker + shifted)
    return sizes[jax.random.permutation(jax.random.fold_in(key, 2), number_of)]


def bell_draw(own_key, extent, deviation, bound, pieces=(), kind=jnp.bfloat16):
    result = jax.random.normal(own_key, extent, jnp.float32) * deviation
    if len(pieces) > 0:
        result = levels(own_key, extent, pieces, -0.22, 0.18) * result
    return jnp.clip(result, min=-bound, max=bound).astype(kind)


def setup_inputs(seed: int = 0) -> dict:
    key_of = jax.random.split(jax.random.key(seed), 6)
    retarded_green_blocks = bell_draw(key_of[0], (SLAB_BLOCKS, ENERGY_SLOTS, 2, BLOCK_ORBITALS, BLOCK_ORBITALS), (2 * BLOCK_ORBITALS) ** -0.5, 0.21875, ((0, 16), (1, 16)))
    contact_lesser_sigma = bell_draw(key_of[1], (SLAB_BLOCKS, ENERGY_SLOTS, 2, BLOCK_ORBITALS, BLOCK_ORBITALS), 1.0, 6.0, ((0, 16), (1, 16)))
    energy_counts = uneven_parts(key_of[2], N_ENERGY, TOTAL, NE_DEV, 1).astype(jnp.int32)
    phonon_shift = place_ends(jax.random.randint(key_of[3], (NW,), 1, TOTAL // 2 + 1), jax.random.fold_in(key_of[3], 1), 1, (TOTAL // 2 + 1) - 1).astype(jnp.int32)
    phonon_weight = jnp.clip(jnp.exp(jax.random.uniform(key_of[4], (4, NW), jnp.float32, math.log(0.01), math.log(0.1))), 0.01, 0.1)
    return dict(retarded_green_blocks=retarded_green_blocks, contact_lesser_sigma=contact_lesser_sigma, energy_counts=energy_counts, phonon_shift=phonon_shift, phonon_weight=phonon_weight)


def complex_product(left, right):
    prods = jnp.einsum("spik,sqkj->spqij", left.astype(jnp.float32), right.astype(jnp.float32))
    return jnp.stack([prods[:, 0, 0] - prods[:, 1, 1], prods[:, 0, 1] + prods[:, 1, 0]], axis=1)


def product_adjoint(left, right):
    prods = jnp.einsum("spik,sqjk->spqij", left.astype(jnp.float32), right.astype(jnp.float32))
    return jnp.stack([prods[:, 0, 0] + prods[:, 1, 1], prods[:, 1, 0] - prods[:, 0, 1]], axis=1)


def kernels(energy_counts, phonon_shift, phonon_weight, groups, per_group):
    total_slots = groups * per_group
    starts = (jnp.cumsum(energy_counts) - energy_counts).astype(jnp.int32)
    slot_numbers = jnp.arange(total_slots, dtype=jnp.int32)
    owner = slot_numbers // per_group
    within = slot_numbers % per_group
    energy_index = starts[owner] + within
    live = (within < energy_counts[owner]).astype(jnp.float32)
    spacing = energy_index[None, :] - energy_index[:, None]
    upward = (spacing[:, :, None] == phonon_shift[None, None, :]).astype(jnp.float32)
    downward = (spacing[:, :, None] == -phonon_shift[None, None, :]).astype(jnp.float32)
    mask = live[:, None] * live[None, :]
    own_kernel = jnp.sum(upward * phonon_weight[0] + downward * phonon_weight[1], axis=-1) * mask
    side_kernel = jnp.sum(upward * phonon_weight[2] + downward * phonon_weight[3], axis=-1) * mask
    return own_kernel.astype(jnp.bfloat16), side_kernel.astype(jnp.bfloat16)


def reference(retarded_green_blocks, contact_lesser_sigma, energy_counts, phonon_shift, phonon_weight):
    own_kernel, side_kernel = kernels(energy_counts, phonon_shift, phonon_weight, N_ENERGY, NE_DEV)

    def dyson(pair):
        retarded, lesser_in = pair
        mixed = complex_product(retarded, lesser_in).astype(jnp.bfloat16)
        return product_adjoint(mixed, retarded).astype(jnp.bfloat16)

    lesser = lax.map(dyson, (retarded_green_blocks, contact_lesser_sigma))
    blank = jnp.zeros_like(lesser[:1])
    padded = jnp.concatenate([blank, lesser, blank], axis=0)
    own_f = own_kernel.astype(jnp.float32)
    side_f = side_kernel.astype(jnp.float32)

    def per_block(index):
        below = lax.dynamic_index_in_dim(padded, index, 0, keepdims=False).astype(jnp.float32)
        middle_block = lax.dynamic_index_in_dim(padded, index + 1, 0, keepdims=False).astype(jnp.float32)
        above = lax.dynamic_index_in_dim(padded, index + 2, 0, keepdims=False).astype(jnp.float32)
        sigma = jnp.einsum("jk,kpab->jpab", own_f, middle_block)
        sigma = sigma + jnp.einsum("jk,kpab->jpab", side_f, below) + jnp.einsum("jk,kpab->jpab", side_f, above)
        sigma = sigma.astype(jnp.bfloat16)
        retarded = lax.dynamic_index_in_dim(retarded_green_blocks, index, 0, keepdims=False)
        return complex_product(retarded, sigma).astype(jnp.bfloat16)

    return lax.map(per_block, jnp.arange(retarded_green_blocks.shape[0], dtype=jnp.int32))
```

```python
import functools

import jax
import jax.numpy as jnp
from jax import lax
from jax.experimental import pallas as pl
from jax.experimental.pallas import tpu as pltpu
from jax.sharding import PartitionSpec as P

SPLIT = (32, 16)
TILE = 16
VMEM = 48 << 20


def lesser_kernel(splits, orbitals, r_ref, s_ref, *refs):
    outs, (right, turned) = refs[: len(splits)], refs[len(splits) :]
    n = orbitals
    rr, ri = r_ref[0], r_ref[1]
    sr, si = s_ref[0], s_ref[1]
    left = jnp.concatenate([rr, ri], axis=1)
    right[:n, :n] = sr
    right[:n, n:] = si
    right[n:, :n] = -si
    right[n:, n:] = sr
    turned[:n, :n] = rr
    turned[:n, n:] = ri
    turned[n:, :n] = -ri
    turned[n:, n:] = rr
    mixed = jnp.dot(left, right[...], preferred_element_type=jnp.float32).astype(jnp.bfloat16)
    lesser = lax.dot_general(
        mixed, turned[...], (((1,), (1,)), ((), ())), preferred_element_type=jnp.float32
    ).astype(jnp.bfloat16)
    whole = sum(splits)
    per_part = n // whole
    for part in range(2):
        for i in range(per_part):
            begin = i * whole
            for width, out in zip(splits, outs):
                out[part * per_part + i] = lesser[begin : begin + width, part * n : (part + 1) * n]
                begin += width


def lesser_blocks(retarded, contact, groups, splits):
    slots, _, n, _ = retarded.shape
    spec = pl.BlockSpec((None, 2, n, n), lambda s: (s, 0, 0, 0))
    return pl.pallas_call(
        functools.partial(lesser_kernel, splits, n),
        grid=(slots,),
        in_specs=[spec, spec],
        out_specs=[pl.BlockSpec((groups, None, w, n), lambda s: (0, s, 0, 0)) for w in splits],
        out_shape=[jax.ShapeDtypeStruct((groups, slots, w, n), jnp.bfloat16) for w in splits],
        scratch_shapes=[pltpu.VMEM((2 * n, 2 * n), jnp.bfloat16)] * 2,
        compiler_params=pltpu.CompilerParams(vmem_limit_bytes=VMEM),
        cost_estimate=pl.CostEstimate(
            flops=slots * 16 * n**3, bytes_accessed=slots * 12 * n * n, transcendentals=0
        ),
        name="lesser",
    )(retarded, contact)


def weights_kernel(groups, per_group, counts, shifts, weights, own_ref, side_ref):
    total = groups * per_group

    def axis_of(dim):
        slot = lax.broadcasted_iota(jnp.int32, (total, total), dim)
        owner = jnp.zeros_like(slot)
        for e in range(1, groups):
            owner = owner + (slot >= e * per_group).astype(jnp.int32)
        within = slot - owner * per_group
        before = jnp.zeros_like(slot)
        held = jnp.zeros_like(slot)
        for e in range(groups):
            before = before + jnp.where(owner > e, counts[e], 0)
            held = held + jnp.where(owner == e, counts[e], 0)
        return before + within, within < held

    energy_j, live_j = axis_of(0)
    energy_k, live_k = axis_of(1)
    spacing = energy_k - energy_j

    def add(m, sums):
        own, side = sums
        shift = shifts[m]
        up, down = spacing == shift, spacing == -shift
        own = own + (jnp.where(up, weights[0, m], 0.0) + jnp.where(down, weights[1, m], 0.0))
        side = side + (jnp.where(up, weights[2, m], 0.0) + jnp.where(down, weights[3, m], 0.0))
        return own, side

    blank = jnp.zeros((total, total), jnp.float32)
    own, side = lax.fori_loop(0, shifts.shape[0], add, (blank, blank))
    mask = jnp.logical_and(live_j, live_k)
    big = total * TILE
    spread = (
        lax.broadcasted_iota(jnp.int32, (big, total), 0) // TILE
        == lax.broadcasted_iota(jnp.int32, (big, total), 1)
    ).astype(jnp.bfloat16)
    same = (
        lax.broadcasted_iota(jnp.int32, (big, big), 0) % TILE
        == lax.broadcasted_iota(jnp.int32, (big, big), 1) % TILE
    )
    for kernel, out in ((own, own_ref), (side, side_ref)):
        kernel = jnp.where(mask, kernel, 0.0).astype(jnp.bfloat16)
        tall = jnp.dot(spread, kernel, preferred_element_type=jnp.float32).astype(jnp.bfloat16)
        wide = lax.dot_general(
            tall, spread, (((1,), (1,)), ((), ())), preferred_element_type=jnp.float32
        )
        out[...] = jnp.where(same, wide, 0.0).astype(jnp.bfloat16)


def mixing_weights(counts, shifts, weights, groups, per_group):
    big = groups * per_group * TILE
    shape = jax.ShapeDtypeStruct((big, big), jnp.bfloat16)
    smem = pl.BlockSpec(memory_space=pltpu.SMEM)
    return pl.pallas_call(
        functools.partial(weights_kernel, groups, per_group),
        in_specs=[smem] * 3,
        out_specs=[pl.BlockSpec(memory_space=pltpu.VMEM)] * 2,
        out_shape=[shape, shape],
        compiler_params=pltpu.CompilerParams(vmem_limit_bytes=VMEM),
        cost_estimate=pl.CostEstimate(flops=4 * 10**9, bytes_accessed=10**7, transcendentals=0),
        name="mixing_weights",
    )(counts, shifts, weights)


def mix_kernel(own_ref, side_ref, here, below, above, out):
    slots, rows, n = here.shape

    def flat(ref):
        return ref[...].reshape(slots * rows, n)

    near = flat(below).astype(jnp.float32) + flat(above).astype(jnp.float32)
    sigma = jnp.dot(own_ref[...], flat(here), preferred_element_type=jnp.float32)
    sigma = sigma + jnp.dot(
        side_ref[...], near.astype(jnp.bfloat16), preferred_element_type=jnp.float32
    )
    out[...] = sigma.astype(jnp.bfloat16).reshape(slots, rows, n)


def mix(own, side, here, below, above):
    slots, rows, n = here.shape
    spec = pl.BlockSpec((slots, TILE, n), lambda t: (0, t, 0))
    kept = pl.BlockSpec(own.shape, lambda t: (0, 0))
    return pl.pallas_call(
        mix_kernel,
        grid=(rows // TILE,),
        in_specs=[kept, kept, spec, spec, spec],
        out_specs=spec,
        out_shape=jax.ShapeDtypeStruct(here.shape, jnp.bfloat16),
        compiler_params=pltpu.CompilerParams(vmem_limit_bytes=VMEM),
        cost_estimate=pl.CostEstimate(
            flops=4 * own.shape[0] ** 2 * n * rows // TILE,
            bytes_accessed=8 * slots * rows * n,
            transcendentals=0,
        ),
        name="mix",
    )(own, side, here, below, above)


def scatter_kernel(splits, orbitals, r_ref, *refs):
    parts, out, right = refs[: len(splits)], refs[len(splits)], refs[len(splits) + 1]
    n = orbitals
    whole = sum(splits)
    per_part = n // whole
    for i in range(per_part):
        begin = i * whole
        for width, part in zip(splits, parts):
            real, imag = part[i], part[per_part + i]
            right[begin : begin + width, :n] = real
            right[begin : begin + width, n:] = imag
            right[n + begin : n + begin + width, :n] = -imag
            right[n + begin : n + begin + width, n:] = real
            begin += width
    left = jnp.concatenate([r_ref[0], r_ref[1]], axis=1)
    result = jnp.dot(left, right[...], preferred_element_type=jnp.float32).astype(jnp.bfloat16)
    out[0] = result[:, :n]
    out[1] = result[:, n:]


def scattered_blocks(retarded, parts, splits):
    slots, _, n, _ = retarded.shape
    groups = parts[0].shape[0]
    spec = pl.BlockSpec((None, 2, n, n), lambda s: (s, 0, 0, 0))
    return pl.pallas_call(
        functools.partial(scatter_kernel, splits, n),
        grid=(slots,),
        in_specs=[spec] + [pl.BlockSpec((groups, None, w, n), lambda s: (0, s, 0, 0)) for w in splits],
        out_specs=spec,
        out_shape=jax.ShapeDtypeStruct(retarded.shape, jnp.bfloat16),
        scratch_shapes=[pltpu.VMEM((2 * n, 2 * n), jnp.bfloat16)],
        compiler_params=pltpu.CompilerParams(vmem_limit_bytes=VMEM),
        cost_estimate=pl.CostEstimate(
            flops=slots * 8 * n**3, bytes_accessed=slots * 12 * n * n, transcendentals=0
        ),
        name="scattered",
    )(retarded, *parts)


def on_device(
    retarded_green_blocks, contact_lesser_sigma, energy_counts, phonon_shift, phonon_weight
):
    groups, blocks = lax.axis_size("energy"), lax.axis_size("atoms")
    _, per_group, _, n, _ = retarded_green_blocks.shape
    up = [(i, i + 1) for i in range(blocks - 1)]
    down = [(j, i) for i, j in up]
    retarded = retarded_green_blocks[0]
    lesser = lesser_blocks(retarded, contact_lesser_sigma[0], groups, SPLIT)
    own, side = mixing_weights(energy_counts, phonon_shift, phonon_weight, groups, per_group)
    returned = []
    for part, width in zip(lesser, SPLIT):
        rows = lax.all_to_all(part, "energy", 0, 0, tiled=True)
        rows = rows.reshape(groups * per_group, width, n)
        below = lax.ppermute(rows, "atoms", up)
        above = lax.ppermute(rows, "atoms", down)
        sigma = mix(own, side, rows, below, above).reshape(groups, per_group, width, n)
        returned.append(lax.all_to_all(sigma, "energy", 0, 0, tiled=True))
    return scattered_blocks(retarded, returned, SPLIT)[None]


def solution(mesh):
    in_specs = (
        P("atoms", "energy", None, None, None),
        P("atoms", "energy", None, None, None),
        P(),
        P(),
        P(),
    )
    out_specs = P("atoms", "energy", None, None, None)
    return jax.shard_map(
        on_device, mesh=mesh, in_specs=in_specs, out_specs=out_specs, check_vma=False
    )
```

```python
import functools

import jax
import jax.numpy as jnp
from jax import lax
from jax.experimental import pallas as pl
from jax.experimental.pallas import tpu as pltpu
from jax.sharding import PartitionSpec as P

PARTS = (5, 4)
ROWS, LANES = 16, 128
PACKED, TOTAL = 32, 30
VMEM_SPEC = pl.BlockSpec(memory_space=pltpu.VMEM)
SMEM_SPEC = pl.BlockSpec(memory_space=pltpu.SMEM)
HBM_SPEC = pl.BlockSpec(memory_space=pltpu.HBM)


def params(mib):
    return pltpu.CompilerParams(vmem_limit_bytes=mib << 20)


def cost(flops, size):
    return pl.CostEstimate(flops=int(flops), bytes_accessed=int(size), transcendentals=0)


def tile_shape(tiles):
    return (tiles, ROWS, LANES)


def lesser_kernel(parts, r_hbm, s_hbm, *refs):
    outs = refs[: len(parts)]
    r_buf, s_buf, right, turned, sems = refs[len(parts) :]
    slots, _, n, _ = r_buf.shape
    share = sum(parts)
    where = [(p, t) for p, width in enumerate(parts) for t in range(width)]
    copies = []
    for s in range(slots):
        copies.append(
            (
                pltpu.make_async_copy(r_hbm.at[s], r_buf.at[s], sems.at[s, 0]),
                pltpu.make_async_copy(s_hbm.at[s], s_buf.at[s], sems.at[s, 1]),
            )
        )
        for copy in copies[-1]:
            copy.start()
    for s in range(slots):
        for copy in copies[s]:
            copy.wait()
        rr, ri = r_buf[s, 0], r_buf[s, 1]
        sr, si = s_buf[s, 0], s_buf[s, 1]
        left = jnp.concatenate([rr, ri], axis=1)
        right[:n, :n] = sr
        right[:n, n:] = si
        right[n:, :n] = -si
        right[n:, n:] = sr
        turned[:n, :n] = rr
        turned[:n, n:] = ri
        turned[n:, :n] = -ri
        turned[n:, n:] = rr
        mixed = jnp.dot(left, right[...], preferred_element_type=jnp.float32).astype(jnp.bfloat16)
        lesser = lax.dot_general(
            mixed, turned[...], (((1,), (1,)), ((), ())), preferred_element_type=jnp.float32
        ).astype(jnp.bfloat16)
        at = 0
        for part in range(2):
            for i in range(n // ROWS):
                for lane in range(n // LANES):
                    column = part * n + lane * LANES
                    value = lesser[i * ROWS : (i + 1) * ROWS, column : column + LANES]
                    p, t = where[at % share]
                    outs[p][at // share, s, t] = value
                    at += 1


def lesser_blocks(retarded, contact, groups, parts):
    slots, _, n, _ = retarded.shape
    return pl.pallas_call(
        functools.partial(lesser_kernel, parts),
        in_specs=[HBM_SPEC, HBM_SPEC],
        out_specs=[VMEM_SPEC] * len(parts),
        out_shape=[
            jax.ShapeDtypeStruct((groups, slots) + tile_shape(tiles), jnp.bfloat16)
            for tiles in parts
        ],
        scratch_shapes=[
            pltpu.VMEM(retarded.shape, jnp.bfloat16),
            pltpu.VMEM(retarded.shape, jnp.bfloat16),
            pltpu.VMEM((2 * n, 2 * n), jnp.bfloat16),
            pltpu.VMEM((2 * n, 2 * n), jnp.bfloat16),
            pltpu.SemaphoreType.DMA((slots, 2)),
        ],
        compiler_params=params(61),
        cost_estimate=cost(slots * 16 * n**3, slots * 12 * n * n),
        name="lesser",
    )(retarded, contact)


def weights_kernel(shifts, weights, own_ref, side_ref):
    energy_j = lax.broadcasted_iota(jnp.int32, (PACKED, PACKED), 0)
    energy_k = lax.broadcasted_iota(jnp.int32, (PACKED, PACKED), 1)
    spacing = energy_k - energy_j

    def add(m, sums):
        own, side = sums
        shift = shifts[m]
        up, down = spacing == shift, spacing == -shift
        own = own + (jnp.where(up, weights[0, m], 0.0) + jnp.where(down, weights[1, m], 0.0))
        side = side + (jnp.where(up, weights[2, m], 0.0) + jnp.where(down, weights[3, m], 0.0))
        return own, side

    blank = jnp.zeros((PACKED, PACKED), jnp.float32)
    sums = lax.fori_loop(0, shifts.shape[0], add, (blank, blank))
    mask = jnp.logical_and(energy_j < TOTAL, energy_k < TOTAL)
    big = PACKED * ROWS
    spread = (
        lax.broadcasted_iota(jnp.int32, (big, PACKED), 0) // ROWS
        == lax.broadcasted_iota(jnp.int32, (big, PACKED), 1)
    ).astype(jnp.bfloat16)
    same = (
        lax.broadcasted_iota(jnp.int32, (big, big), 0) % ROWS
        == lax.broadcasted_iota(jnp.int32, (big, big), 1) % ROWS
    )
    for kernel, out in zip(sums, (own_ref, side_ref)):
        kernel = jnp.where(mask, kernel, 0.0).astype(jnp.bfloat16)
        tall = jnp.dot(spread, kernel, preferred_element_type=jnp.float32).astype(jnp.bfloat16)
        wide = lax.dot_general(
            tall, spread, (((1,), (1,)), ((), ())), preferred_element_type=jnp.float32
        )
        out[...] = jnp.where(same, wide, 0.0).astype(jnp.bfloat16)


def mixing_weights(shifts, weights):
    shape = jax.ShapeDtypeStruct((PACKED * ROWS, PACKED * ROWS), jnp.bfloat16)
    return pl.pallas_call(
        weights_kernel,
        in_specs=[SMEM_SPEC, SMEM_SPEC],
        out_specs=[VMEM_SPEC] * 2,
        out_shape=[shape, shape],
        compiler_params=params(16),
        cost_estimate=cost(2 * 10**9, 4 * 10**6),
        name="mixing_weights",
    )(shifts, weights)


def find_starts(counts, starts):
    so_far = jnp.int32(0)
    for e in range(counts.shape[0]):
        starts[e] = so_far
        so_far = so_far + counts[e]


def pack_kernel(counts, rows, *refs):
    outs, starts = refs[:-1], refs[-1]
    find_starts(counts, starts)
    for e in range(rows.shape[0]):
        for s in range(rows.shape[1]):
            row = jnp.where(s < counts[e], starts[e] + s, PACKED - 1)
            begin = 0
            for out in outs:
                out[row] = rows[e, s, begin : begin + out.shape[1]]
                begin += out.shape[1]
    for out in outs:
        for row in range(TOTAL, PACKED):
            out[row] = jnp.zeros(out.shape[1:], out.dtype)


def pack(counts, rows, parts):
    return pl.pallas_call(
        pack_kernel,
        in_specs=[SMEM_SPEC, VMEM_SPEC],
        out_specs=[VMEM_SPEC] * len(parts),
        out_shape=[
            jax.ShapeDtypeStruct((PACKED,) + tile_shape(tiles), jnp.bfloat16) for tiles in parts
        ],
        scratch_shapes=[pltpu.SMEM(counts.shape, jnp.int32)],
        compiler_params=params(4),
        cost_estimate=cost(0, 4 * rows.size),
        name="pack",
    )(counts, rows)


def mix_kernel(counts, own_ref, side_ref, here, below, above, out, sigma, starts):
    find_starts(counts, starts)
    tiles = here.shape[1]

    def flat(value):
        return value.reshape(PACKED * ROWS, LANES)

    centre = jnp.concatenate([flat(here[:, t]) for t in range(tiles)], axis=1)
    near = jnp.concatenate([flat(below[:, t] + above[:, t]) for t in range(tiles)], axis=1)
    total = jnp.dot(own_ref[...], centre, preferred_element_type=jnp.float32)
    total = total + jnp.dot(side_ref[...], near, preferred_element_type=jnp.float32)
    total = total.astype(jnp.bfloat16)
    for t in range(tiles):
        sigma[:, t] = total[:, t * LANES : (t + 1) * LANES].reshape(PACKED, ROWS, LANES)
    for e in range(out.shape[0]):
        for s in range(out.shape[1]):
            row = jnp.where(s < counts[e], starts[e] + s, PACKED - 1)
            out[e, s] = sigma[row]


def mix(counts, own, side, here, below, above, slots):
    tiles = here.shape[1]
    groups = counts.shape[0]
    return pl.pallas_call(
        mix_kernel,
        in_specs=[SMEM_SPEC] + [VMEM_SPEC] * 5,
        out_specs=VMEM_SPEC,
        out_shape=jax.ShapeDtypeStruct((groups, slots) + tile_shape(tiles), jnp.bfloat16),
        scratch_shapes=[
            pltpu.VMEM(here.shape, jnp.bfloat16),
            pltpu.SMEM(counts.shape, jnp.int32),
        ],
        compiler_params=params(16),
        cost_estimate=cost(4 * own.size * tiles * LANES, 6 * here.size),
        name="mix",
    )(counts, own, side, here, below, above)


def scatter_kernel(parts, *refs):
    received, (r_ref, out_hbm, right, result, sems) = refs[: len(parts)], refs[len(parts) :]
    slots, _, n, _ = r_ref.shape
    share = sum(parts)
    where = [(p, t) for p, width in enumerate(parts) for t in range(width)]
    copies = []
    for s in range(slots):
        at = 0
        for part in range(2):
            for i in range(n // ROWS):
                for lane in range(n // LANES):
                    p, t = where[at % share]
                    value = received[p][at // share, s, t]
                    row, column = i * ROWS, lane * LANES
                    first, second = (column, n + column) if part == 0 else (n + column, column)
                    right[row : row + ROWS, first : first + LANES] = value
                    value = value if part == 0 else -value
                    right[n + row : n + row + ROWS, second : second + LANES] = value
                    at += 1
        left = jnp.concatenate([r_ref[s, 0], r_ref[s, 1]], axis=1)
        product = jnp.dot(left, right[...], preferred_element_type=jnp.float32)
        product = product.astype(jnp.bfloat16)
        result[s, 0] = product[:, :n]
        result[s, 1] = product[:, n:]
        copy = pltpu.make_async_copy(result.at[s], out_hbm.at[s], sems.at[s])
        copy.start()
        copies.append(copy)
    for copy in copies:
        copy.wait()


def scattered_blocks(retarded, received, parts):
    slots, _, n, _ = retarded.shape
    return pl.pallas_call(
        functools.partial(scatter_kernel, parts),
        in_specs=[VMEM_SPEC] * (len(parts) + 1),
        out_specs=HBM_SPEC,
        out_shape=jax.ShapeDtypeStruct(retarded.shape, jnp.bfloat16),
        scratch_shapes=[
            pltpu.VMEM((2 * n, 2 * n), jnp.bfloat16),
            pltpu.VMEM(retarded.shape, jnp.bfloat16),
            pltpu.SemaphoreType.DMA((slots,)),
        ],
        compiler_params=params(32),
        cost_estimate=cost(slots * 8 * n**3, slots * 12 * n * n),
        name="scattered",
    )(*received, retarded)


def on_device(
    retarded_green_blocks, contact_lesser_sigma, energy_counts, phonon_shift, phonon_weight
):
    groups, blocks = lax.axis_size("energy"), lax.axis_size("atoms")
    slots = retarded_green_blocks.shape[1]
    up = [(i, i + 1) for i in range(blocks - 1)]
    down = [(j, i) for i, j in up]
    retarded = retarded_green_blocks[0]
    lesser = lesser_blocks(retarded, contact_lesser_sigma[0], groups, PARTS)
    own, side = mixing_weights(phonon_shift, phonon_weight)
    returned = []
    for part, tiles in zip(lesser, PARTS):
        rows = lax.all_to_all(part, "energy", 0, 0, tiled=True)
        (here,) = pack(energy_counts, rows, (tiles,))
        below = lax.ppermute(here, "atoms", up)
        above = lax.ppermute(here, "atoms", down)
        sigma = mix(energy_counts, own, side, here, below, above, slots)
        returned.append(lax.all_to_all(sigma, "energy", 0, 0, tiled=True))
    return scattered_blocks(retarded, returned, PARTS)[None]


def solution(mesh):
    in_specs = (
        P("atoms", "energy", None, None, None),
        P("atoms", "energy", None, None, None),
        P(),
        P(),
        P(),
    )
    out_specs = P("atoms", "energy", None, None, None)
    return jax.shard_map(
        on_device, mesh=mesh, in_specs=in_specs, out_specs=out_specs, check_vma=False
    )
```

```python
import functools

import jax
import jax.numpy as jnp
from jax import lax
from jax.experimental import pallas as pl
from jax.experimental.pallas import tpu as pltpu
from jax.sharding import PartitionSpec as P

PARTS = (5, 4)
ROWS, LANES = 16, 128
LANE_TILES = 3
LIMIT = 61
PACKED, TOTAL = 32, 30
VMEM_SPEC = pl.BlockSpec(memory_space=pltpu.VMEM)
SMEM_SPEC = pl.BlockSpec(memory_space=pltpu.SMEM)
HBM_SPEC = pl.BlockSpec(memory_space=pltpu.HBM)


def params(mib):
    return pltpu.CompilerParams(vmem_limit_bytes=mib << 20)


def cost(flops, size):
    return pl.CostEstimate(flops=int(flops), bytes_accessed=int(size), transcendentals=0)


def tile_shape(tiles):
    return (tiles, ROWS, LANES)


def homes(parts, groups):
    found, at = [], 0
    across = 2 * LANE_TILES
    for width in parts:
        held = []
        for index in range(width * groups):
            row, rest = divmod(at, across)
            held.append((index // width, index % width, row, rest // LANE_TILES, rest % LANE_TILES))
            at += 1
        found.append(held)
    return found


def lesser_kernel(held, r_hbm, s_hbm, out, r_buf, s_buf, right, turned, sems):
    slots, _, n, _ = r_buf.shape
    first, last = held[0][2] * ROWS, (held[-1][2] + 1) * ROWS
    copies = []
    for s in range(slots):
        copies.append(
            (
                pltpu.make_async_copy(r_hbm.at[s], r_buf.at[s], sems.at[s, 0]),
                pltpu.make_async_copy(s_hbm.at[s], s_buf.at[s], sems.at[s, 1]),
            )
        )
        for copy in copies[-1]:
            copy.start()
    for s in range(slots):
        for copy in copies[s]:
            copy.wait()
        rr, ri = r_buf[s, 0], r_buf[s, 1]
        sr, si = s_buf[s, 0], s_buf[s, 1]
        left = jnp.concatenate([rr[first:last], ri[first:last]], axis=1)
        right[:n, :n] = sr
        right[:n, n:] = si
        right[n:, :n] = -si
        right[n:, n:] = sr
        turned[:n, :n] = rr
        turned[:n, n:] = ri
        turned[n:, :n] = -ri
        turned[n:, n:] = rr
        mixed = jnp.dot(left, right[...], preferred_element_type=jnp.float32).astype(jnp.bfloat16)
        lesser = lax.dot_general(
            mixed, turned[...], (((1,), (1,)), ((), ())), preferred_element_type=jnp.float32
        ).astype(jnp.bfloat16)
        for owner, t, row, half, lane in held:
            top, column = row * ROWS - first, half * n + lane * LANES
            out[owner, s, t] = lesser[top : top + ROWS, column : column + LANES]


def lesser_blocks(retarded, contact, groups, held):
    slots, _, n, _ = retarded.shape
    tiles = len(held) // groups
    return pl.pallas_call(
        functools.partial(lesser_kernel, held),
        in_specs=[HBM_SPEC, HBM_SPEC],
        out_specs=VMEM_SPEC,
        out_shape=jax.ShapeDtypeStruct((groups, slots) + tile_shape(tiles), jnp.bfloat16),
        scratch_shapes=[
            pltpu.VMEM(retarded.shape, jnp.bfloat16),
            pltpu.VMEM(retarded.shape, jnp.bfloat16),
            pltpu.VMEM((2 * n, 2 * n), jnp.bfloat16),
            pltpu.VMEM((2 * n, 2 * n), jnp.bfloat16),
            pltpu.SemaphoreType.DMA((slots, 2)),
        ],
        compiler_params=params(LIMIT),
        cost_estimate=cost(slots * 8 * n**3, slots * 12 * n * n),
        name="lesser",
    )(retarded, contact)


def weights_kernel(shifts, weights, own_ref, side_ref):
    energy_j = lax.broadcasted_iota(jnp.int32, (PACKED, PACKED), 0)
    energy_k = lax.broadcasted_iota(jnp.int32, (PACKED, PACKED), 1)
    spacing = energy_k - energy_j

    def add(m, sums):
        own, side = sums
        shift = shifts[m]
        up, down = spacing == shift, spacing == -shift
        own = own + (jnp.where(up, weights[0, m], 0.0) + jnp.where(down, weights[1, m], 0.0))
        side = side + (jnp.where(up, weights[2, m], 0.0) + jnp.where(down, weights[3, m], 0.0))
        return own, side

    blank = jnp.zeros((PACKED, PACKED), jnp.float32)
    sums = lax.fori_loop(0, shifts.shape[0], add, (blank, blank))
    mask = jnp.logical_and(energy_j < TOTAL, energy_k < TOTAL)
    big = PACKED * ROWS
    spread = (
        lax.broadcasted_iota(jnp.int32, (big, PACKED), 0) // ROWS
        == lax.broadcasted_iota(jnp.int32, (big, PACKED), 1)
    ).astype(jnp.bfloat16)
    same = (
        lax.broadcasted_iota(jnp.int32, (big, big), 0) % ROWS
        == lax.broadcasted_iota(jnp.int32, (big, big), 1) % ROWS
    )
    for kernel, out in zip(sums, (own_ref, side_ref)):
        kernel = jnp.where(mask, kernel, 0.0).astype(jnp.bfloat16)
        tall = jnp.dot(spread, kernel, preferred_element_type=jnp.float32).astype(jnp.bfloat16)
        wide = lax.dot_general(
            tall, spread, (((1,), (1,)), ((), ())), preferred_element_type=jnp.float32
        )
        out[...] = jnp.where(same, wide, 0.0).astype(jnp.bfloat16)


def mixing_weights(shifts, weights):
    shape = jax.ShapeDtypeStruct((PACKED * ROWS, PACKED * ROWS), jnp.bfloat16)
    return pl.pallas_call(
        weights_kernel,
        in_specs=[SMEM_SPEC, SMEM_SPEC],
        out_specs=[VMEM_SPEC] * 2,
        out_shape=[shape, shape],
        compiler_params=params(16),
        cost_estimate=cost(2 * 10**9, 4 * 10**6),
        name="mixing_weights",
    )(shifts, weights)


def find_starts(counts, starts):
    so_far = jnp.int32(0)
    for e in range(counts.shape[0]):
        starts[e] = so_far
        so_far = so_far + counts[e]


def pack_kernel(counts, rows, *refs):
    outs, starts = refs[:-1], refs[-1]
    find_starts(counts, starts)
    for e in range(rows.shape[0]):
        for s in range(rows.shape[1]):
            row = jnp.where(s < counts[e], starts[e] + s, PACKED - 1)
            begin = 0
            for out in outs:
                out[row] = rows[e, s, begin : begin + out.shape[1]]
                begin += out.shape[1]
    for out in outs:
        for row in range(TOTAL, PACKED):
            out[row] = jnp.zeros(out.shape[1:], out.dtype)


def pack(counts, rows, parts):
    return pl.pallas_call(
        pack_kernel,
        in_specs=[SMEM_SPEC, VMEM_SPEC],
        out_specs=[VMEM_SPEC] * len(parts),
        out_shape=[
            jax.ShapeDtypeStruct((PACKED,) + tile_shape(tiles), jnp.bfloat16) for tiles in parts
        ],
        scratch_shapes=[pltpu.SMEM(counts.shape, jnp.int32)],
        compiler_params=params(4),
        cost_estimate=cost(0, 4 * rows.size),
        name="pack",
    )(counts, rows)


def mix_kernel(counts, own_ref, side_ref, here, below, above, out, sigma, starts):
    find_starts(counts, starts)
    tiles = here.shape[1]

    def flat(value):
        return value.reshape(PACKED * ROWS, LANES)

    centre = jnp.concatenate([flat(here[:, t]) for t in range(tiles)], axis=1)
    near = jnp.concatenate([flat(below[:, t] + above[:, t]) for t in range(tiles)], axis=1)
    total = jnp.dot(own_ref[...], centre, preferred_element_type=jnp.float32)
    total = total + jnp.dot(side_ref[...], near, preferred_element_type=jnp.float32)
    total = total.astype(jnp.bfloat16)
    for t in range(tiles):
        sigma[:, t] = total[:, t * LANES : (t + 1) * LANES].reshape(PACKED, ROWS, LANES)
    for e in range(out.shape[0]):
        for s in range(out.shape[1]):
            row = jnp.where(s < counts[e], starts[e] + s, PACKED - 1)
            out[e, s] = sigma[row]


def mix(counts, own, side, here, below, above, slots):
    tiles = here.shape[1]
    groups = counts.shape[0]
    return pl.pallas_call(
        mix_kernel,
        in_specs=[SMEM_SPEC] + [VMEM_SPEC] * 5,
        out_specs=VMEM_SPEC,
        out_shape=jax.ShapeDtypeStruct((groups, slots) + tile_shape(tiles), jnp.bfloat16),
        scratch_shapes=[
            pltpu.VMEM(here.shape, jnp.bfloat16),
            pltpu.SMEM(counts.shape, jnp.int32),
        ],
        compiler_params=params(16),
        cost_estimate=cost(4 * own.size * tiles * LANES, 6 * here.size),
        name="mix",
    )(counts, own, side, here, below, above)


def scatter_kernel(parts, *refs):
    received, (r_ref, out_hbm, right, result, sems) = refs[: len(parts)], refs[len(parts) :]
    slots, _, n, _ = r_ref.shape
    found = homes(parts, received[0].shape[0])
    copies = []
    for s in range(slots):
        for held, part in zip(found, received):
            for owner, t, tile, half, lane in held:
                value = part[owner, s, t]
                row, column = tile * ROWS, lane * LANES
                first, second = (column, n + column) if half == 0 else (n + column, column)
                right[row : row + ROWS, first : first + LANES] = value
                value = value if half == 0 else -value
                right[n + row : n + row + ROWS, second : second + LANES] = value
        left = jnp.concatenate([r_ref[s, 0], r_ref[s, 1]], axis=1)
        product = jnp.dot(left, right[...], preferred_element_type=jnp.float32)
        product = product.astype(jnp.bfloat16)
        result[s, 0] = product[:, :n]
        result[s, 1] = product[:, n:]
        copy = pltpu.make_async_copy(result.at[s], out_hbm.at[s], sems.at[s])
        copy.start()
        copies.append(copy)
    for copy in copies:
        copy.wait()


def scattered_blocks(retarded, received, parts):
    slots, _, n, _ = retarded.shape
    return pl.pallas_call(
        functools.partial(scatter_kernel, parts),
        in_specs=[VMEM_SPEC] * (len(parts) + 1),
        out_specs=HBM_SPEC,
        out_shape=jax.ShapeDtypeStruct(retarded.shape, jnp.bfloat16),
        scratch_shapes=[
            pltpu.VMEM((2 * n, 2 * n), jnp.bfloat16),
            pltpu.VMEM(retarded.shape, jnp.bfloat16),
            pltpu.SemaphoreType.DMA((slots,)),
        ],
        compiler_params=params(32),
        cost_estimate=cost(slots * 8 * n**3, slots * 12 * n * n),
        name="scattered",
    )(*received, retarded)


def on_device(
    retarded_green_blocks, contact_lesser_sigma, energy_counts, phonon_shift, phonon_weight
):
    groups, blocks = lax.axis_size("energy"), lax.axis_size("atoms")
    slots = retarded_green_blocks.shape[1]
    up = [(i, i + 1) for i in range(blocks - 1)]
    down = [(j, i) for i, j in up]
    retarded = retarded_green_blocks[0]
    found = homes(PARTS, groups)
    own, side = mixing_weights(phonon_shift, phonon_weight)
    returned = []
    for held, tiles in zip(found, PARTS):
        lesser = lesser_blocks(retarded, contact_lesser_sigma[0], groups, held)
        rows = lax.all_to_all(lesser, "energy", 0, 0, tiled=True)
        (here,) = pack(energy_counts, rows, (tiles,))
        below = lax.ppermute(here, "atoms", up)
        above = lax.ppermute(here, "atoms", down)
        sigma = mix(energy_counts, own, side, here, below, above, slots)
        returned.append(lax.all_to_all(sigma, "energy", 0, 0, tiled=True))
    return scattered_blocks(retarded, returned, PARTS)[None]


def solution(mesh):
    in_specs = (
        P("atoms", "energy", None, None, None),
        P("atoms", "energy", None, None, None),
        P(),
        P(),
        P(),
    )
    out_specs = P("atoms", "energy", None, None, None)
    return jax.shard_map(
        on_device, mesh=mesh, in_specs=in_specs, out_specs=out_specs, check_vma=False
    )
```

```python
import functools

import jax
import jax.numpy as jnp
from jax import lax
from jax.experimental import pallas as pl
from jax.experimental.pallas import tpu as pltpu
from jax.sharding import PartitionSpec as P

PARTS = (5, 4)
ROWS, LANES = 16, 128
LANE_TILES = 3
LIMIT = 61
TOTAL = 30
VMEM_SPEC = pl.BlockSpec(memory_space=pltpu.VMEM)
SMEM_SPEC = pl.BlockSpec(memory_space=pltpu.SMEM)
HBM_SPEC = pl.BlockSpec(memory_space=pltpu.HBM)


def params(mib):
    return pltpu.CompilerParams(vmem_limit_bytes=mib << 20)


def cost(flops, size):
    return pl.CostEstimate(flops=int(flops), bytes_accessed=int(size), transcendentals=0)


def tile_shape(tiles):
    return (tiles, ROWS, LANES)


def homes(parts, groups):
    found, at = [], 0
    across = 2 * LANE_TILES
    for width in parts:
        held = []
        for index in range(width * groups):
            row, rest = divmod(at, across)
            held.append((index // width, index % width, row, rest // LANE_TILES, rest % LANE_TILES))
            at += 1
        found.append(held)
    return found


def lesser_kernel(held, r_hbm, s_hbm, out, r_buf, s_buf, right, turned, sems):
    slots, _, n, _ = r_buf.shape
    first, last = held[0][2] * ROWS, (held[-1][2] + 1) * ROWS
    copies = []
    for s in range(slots):
        copies.append(
            (
                pltpu.make_async_copy(r_hbm.at[s], r_buf.at[s], sems.at[s, 0]),
                pltpu.make_async_copy(s_hbm.at[s], s_buf.at[s], sems.at[s, 1]),
            )
        )
        for copy in copies[-1]:
            copy.start()
    for s in range(slots):
        for copy in copies[s]:
            copy.wait()
        rr, ri = r_buf[s, 0], r_buf[s, 1]
        sr, si = s_buf[s, 0], s_buf[s, 1]
        left = jnp.concatenate([rr[first:last], ri[first:last]], axis=1)
        right[:n, :n] = sr
        right[:n, n:] = si
        right[n:, :n] = -si
        right[n:, n:] = sr
        turned[:n, :n] = rr
        turned[:n, n:] = ri
        turned[n:, :n] = -ri
        turned[n:, n:] = rr
        mixed = jnp.dot(left, right[...], preferred_element_type=jnp.float32).astype(jnp.bfloat16)
        lesser = lax.dot_general(
            mixed, turned[...], (((1,), (1,)), ((), ())), preferred_element_type=jnp.float32
        ).astype(jnp.bfloat16)
        for owner, t, row, half, lane in held:
            top, column = row * ROWS - first, half * n + lane * LANES
            out[owner, s, t] = lesser[top : top + ROWS, column : column + LANES]


def lesser_blocks(retarded, contact, groups, held):
    slots, _, n, _ = retarded.shape
    tiles = len(held) // groups
    return pl.pallas_call(
        functools.partial(lesser_kernel, held),
        in_specs=[HBM_SPEC, HBM_SPEC],
        out_specs=VMEM_SPEC,
        out_shape=jax.ShapeDtypeStruct((groups, slots) + tile_shape(tiles), jnp.bfloat16),
        scratch_shapes=[
            pltpu.VMEM(retarded.shape, jnp.bfloat16),
            pltpu.VMEM(retarded.shape, jnp.bfloat16),
            pltpu.VMEM((2 * n, 2 * n), jnp.bfloat16),
            pltpu.VMEM((2 * n, 2 * n), jnp.bfloat16),
            pltpu.SemaphoreType.DMA((slots, 2)),
        ],
        compiler_params=params(LIMIT),
        cost_estimate=cost(slots * 8 * n**3, slots * 12 * n * n),
        name="lesser",
    )(retarded, contact)


def weights_kernel(shifts, weights, own_ref, side_ref):
    energy_j = lax.broadcasted_iota(jnp.int32, (TOTAL, TOTAL), 0)
    energy_k = lax.broadcasted_iota(jnp.int32, (TOTAL, TOTAL), 1)
    spacing = energy_k - energy_j

    def add(m, sums):
        own, side = sums
        shift = shifts[m]
        up, down = spacing == shift, spacing == -shift
        own = own + (jnp.where(up, weights[0, m], 0.0) + jnp.where(down, weights[1, m], 0.0))
        side = side + (jnp.where(up, weights[2, m], 0.0) + jnp.where(down, weights[3, m], 0.0))
        return own, side

    blank = jnp.zeros((TOTAL, TOTAL), jnp.float32)
    sums = lax.fori_loop(0, shifts.shape[0], add, (blank, blank))
    big = TOTAL * ROWS
    spread = (
        lax.broadcasted_iota(jnp.int32, (big, TOTAL), 0) // ROWS
        == lax.broadcasted_iota(jnp.int32, (big, TOTAL), 1)
    ).astype(jnp.bfloat16)
    same = (
        lax.broadcasted_iota(jnp.int32, (big, big), 0) % ROWS
        == lax.broadcasted_iota(jnp.int32, (big, big), 1) % ROWS
    )
    for kernel, out in zip(sums, (own_ref, side_ref)):
        kernel = kernel.astype(jnp.bfloat16)
        tall = jnp.dot(spread, kernel, preferred_element_type=jnp.float32).astype(jnp.bfloat16)
        wide = lax.dot_general(
            tall, spread, (((1,), (1,)), ((), ())), preferred_element_type=jnp.float32
        )
        out[...] = jnp.where(same, wide, 0.0).astype(jnp.bfloat16)


def mixing_weights(shifts, weights):
    shape = jax.ShapeDtypeStruct((TOTAL * ROWS, TOTAL * ROWS), jnp.bfloat16)
    return pl.pallas_call(
        weights_kernel,
        in_specs=[SMEM_SPEC, SMEM_SPEC],
        out_specs=[VMEM_SPEC] * 2,
        out_shape=[shape, shape],
        compiler_params=params(16),
        cost_estimate=cost(2 * 10**9, 4 * 10**6),
        name="mixing_weights",
    )(shifts, weights)


def find_starts(counts, starts):
    so_far = jnp.int32(0)
    for e in range(counts.shape[0]):
        starts[e] = so_far
        so_far = so_far + counts[e]


def pack_kernel(counts, rows, out, starts):
    find_starts(counts, starts)
    for e in range(rows.shape[0]):
        for s in reversed(range(rows.shape[1])):
            row = starts[e] + jnp.where(s < counts[e], s, 0)
            out[row] = rows[e, s]


def pack(counts, rows):
    tiles = rows.shape[2]
    return pl.pallas_call(
        pack_kernel,
        in_specs=[SMEM_SPEC, VMEM_SPEC],
        out_specs=VMEM_SPEC,
        out_shape=jax.ShapeDtypeStruct((TOTAL,) + tile_shape(tiles), jnp.bfloat16),
        scratch_shapes=[pltpu.SMEM(counts.shape, jnp.int32)],
        compiler_params=params(4),
        cost_estimate=cost(0, 4 * rows.size),
        name="pack",
    )(counts, rows)


def mix_kernel(counts, own_ref, side_ref, here, below, above, out, sigma, starts):
    find_starts(counts, starts)
    tiles = here.shape[1]

    def flat(value):
        return value.reshape(TOTAL * ROWS, LANES)

    centre = jnp.concatenate([flat(here[:, t]) for t in range(tiles)], axis=1)
    near = jnp.concatenate([flat(below[:, t] + above[:, t]) for t in range(tiles)], axis=1)
    total = jnp.dot(own_ref[...], centre, preferred_element_type=jnp.float32)
    total = total + jnp.dot(side_ref[...], near, preferred_element_type=jnp.float32)
    total = total.astype(jnp.bfloat16)
    for t in range(tiles):
        sigma[:TOTAL, t] = total[:, t * LANES : (t + 1) * LANES].reshape(TOTAL, ROWS, LANES)
    sigma[TOTAL] = jnp.zeros(sigma.shape[1:], sigma.dtype)
    for e in range(out.shape[0]):
        for s in range(out.shape[1]):
            row = jnp.where(s < counts[e], starts[e] + s, TOTAL)
            out[e, s] = sigma[row]


def mix(counts, own, side, here, below, above, slots):
    tiles = here.shape[1]
    groups = counts.shape[0]
    return pl.pallas_call(
        mix_kernel,
        in_specs=[SMEM_SPEC] + [VMEM_SPEC] * 5,
        out_specs=VMEM_SPEC,
        out_shape=jax.ShapeDtypeStruct((groups, slots) + tile_shape(tiles), jnp.bfloat16),
        scratch_shapes=[
            pltpu.VMEM((TOTAL + 1,) + here.shape[1:], jnp.bfloat16),
            pltpu.SMEM(counts.shape, jnp.int32),
        ],
        compiler_params=params(16),
        cost_estimate=cost(4 * own.size * tiles * LANES, 6 * here.size),
        name="mix",
    )(counts, own, side, here, below, above)


def scatter_kernel(parts, *refs):
    received, (r_ref, out_hbm, right, result, sems) = refs[: len(parts)], refs[len(parts) :]
    slots, _, n, _ = r_ref.shape
    found = homes(parts, received[0].shape[0])
    copies = []
    for s in range(slots):
        for held, part in zip(found, received):
            for owner, t, tile, half, lane in held:
                value = part[owner, s, t]
                row, column = tile * ROWS, lane * LANES
                first, second = (column, n + column) if half == 0 else (n + column, column)
                right[row : row + ROWS, first : first + LANES] = value
                value = value if half == 0 else -value
                right[n + row : n + row + ROWS, second : second + LANES] = value
        left = jnp.concatenate([r_ref[s, 0], r_ref[s, 1]], axis=1)
        product = jnp.dot(left, right[...], preferred_element_type=jnp.float32)
        product = product.astype(jnp.bfloat16)
        result[s, 0] = product[:, :n]
        result[s, 1] = product[:, n:]
        copy = pltpu.make_async_copy(result.at[s], out_hbm.at[s], sems.at[s])
        copy.start()
        copies.append(copy)
    for copy in copies:
        copy.wait()


def scattered_blocks(retarded, received, parts):
    slots, _, n, _ = retarded.shape
    return pl.pallas_call(
        functools.partial(scatter_kernel, parts),
        in_specs=[VMEM_SPEC] * (len(parts) + 1),
        out_specs=HBM_SPEC,
        out_shape=jax.ShapeDtypeStruct(retarded.shape, jnp.bfloat16),
        scratch_shapes=[
            pltpu.VMEM((2 * n, 2 * n), jnp.bfloat16),
            pltpu.VMEM(retarded.shape, jnp.bfloat16),
            pltpu.SemaphoreType.DMA((slots,)),
        ],
        compiler_params=params(32),
        cost_estimate=cost(slots * 8 * n**3, slots * 12 * n * n),
        name="scattered",
    )(*received, retarded)


def on_device(
    retarded_green_blocks, contact_lesser_sigma, energy_counts, phonon_shift, phonon_weight
):
    groups, blocks = lax.axis_size("energy"), lax.axis_size("atoms")
    slots = retarded_green_blocks.shape[1]
    up = [(i, i + 1) for i in range(blocks - 1)]
    down = [(j, i) for i, j in up]
    retarded = retarded_green_blocks[0]
    found = homes(PARTS, groups)
    own, side = mixing_weights(phonon_shift, phonon_weight)
    returned = []
    for held in found:
        lesser = lesser_blocks(retarded, contact_lesser_sigma[0], groups, held)
        rows = lax.all_to_all(lesser, "energy", 0, 0, tiled=True)
        here = pack(energy_counts, rows)
        below = lax.ppermute(here, "atoms", up)
        above = lax.ppermute(here, "atoms", down)
        sigma = mix(energy_counts, own, side, here, below, above, slots)
        returned.append(lax.all_to_all(sigma, "energy", 0, 0, tiled=True))
    return scattered_blocks(retarded, returned, PARTS)[None]


def solution(mesh):
    in_specs = (
        P("atoms", "energy", None, None, None),
        P("atoms", "energy", None, None, None),
        P(),
        P(),
        P(),
    )
    out_specs = P("atoms", "energy", None, None, None)
    return jax.shard_map(
        on_device, mesh=mesh, in_specs=in_specs, out_specs=out_specs, check_vma=False
    )
```

```python
import functools

import jax
import jax.numpy as jnp
from jax import lax
from jax.experimental import pallas as pl
from jax.experimental.pallas import tpu as pltpu
from jax.sharding import PartitionSpec as P

PARTS = (4, 5)
ROWS, LANES = 16, 128
LANE_TILES = 3
LIMIT = 61
TOTAL = 30
VMEM_SPEC = pl.BlockSpec(memory_space=pltpu.VMEM)
SMEM_SPEC = pl.BlockSpec(memory_space=pltpu.SMEM)
HBM_SPEC = pl.BlockSpec(memory_space=pltpu.HBM)


def params(mib):
    return pltpu.CompilerParams(vmem_limit_bytes=mib << 20)


def cost(flops, size):
    return pl.CostEstimate(flops=int(flops), bytes_accessed=int(size), transcendentals=0)


def tile_shape(tiles):
    return (tiles, ROWS, LANES)


def homes(parts, groups):
    found, at = [], 0
    across = 2 * LANE_TILES
    for width in parts:
        held = []
        for index in range(width * groups):
            row, rest = divmod(at, across)
            held.append((index // width, index % width, row, rest // LANE_TILES, rest % LANE_TILES))
            at += 1
        found.append(held)
    return found


def lesser_kernel(held, r_hbm, s_hbm, out, r_buf, s_buf, right, turned, sems):
    slots, _, n, _ = r_buf.shape
    first, last = held[0][2] * ROWS, (held[-1][2] + 1) * ROWS
    copies = []
    for s in range(slots):
        copies.append(
            (
                pltpu.make_async_copy(r_hbm.at[s], r_buf.at[s], sems.at[s, 0]),
                pltpu.make_async_copy(s_hbm.at[s], s_buf.at[s], sems.at[s, 1]),
            )
        )
        for copy in copies[-1]:
            copy.start()
    for s in range(slots):
        for copy in copies[s]:
            copy.wait()
        rr, ri = r_buf[s, 0], r_buf[s, 1]
        sr, si = s_buf[s, 0], s_buf[s, 1]
        left = jnp.concatenate([rr[first:last], ri[first:last]], axis=1)
        right[:n, :n] = sr
        right[:n, n:] = si
        right[n:, :n] = -si
        right[n:, n:] = sr
        turned[:n, :n] = rr
        turned[:n, n:] = ri
        turned[n:, :n] = -ri
        turned[n:, n:] = rr
        mixed = jnp.dot(left, right[...], preferred_element_type=jnp.float32).astype(jnp.bfloat16)
        lesser = lax.dot_general(
            mixed, turned[...], (((1,), (1,)), ((), ())), preferred_element_type=jnp.float32
        ).astype(jnp.bfloat16)
        for owner, t, row, half, lane in held:
            top, column = row * ROWS - first, half * n + lane * LANES
            out[owner, s, t] = lesser[top : top + ROWS, column : column + LANES]


def lesser_blocks(retarded, contact, groups, held):
    slots, _, n, _ = retarded.shape
    tiles = len(held) // groups
    return pl.pallas_call(
        functools.partial(lesser_kernel, held),
        in_specs=[HBM_SPEC, HBM_SPEC],
        out_specs=VMEM_SPEC,
        out_shape=jax.ShapeDtypeStruct((groups, slots) + tile_shape(tiles), jnp.bfloat16),
        scratch_shapes=[
            pltpu.VMEM(retarded.shape, jnp.bfloat16),
            pltpu.VMEM(retarded.shape, jnp.bfloat16),
            pltpu.VMEM((2 * n, 2 * n), jnp.bfloat16),
            pltpu.VMEM((2 * n, 2 * n), jnp.bfloat16),
            pltpu.SemaphoreType.DMA((slots, 2)),
        ],
        compiler_params=params(LIMIT),
        cost_estimate=cost(slots * 8 * n**3, slots * 12 * n * n),
        name="lesser",
    )(retarded, contact)


def weights_kernel(shifts, weights, own_ref, side_ref):
    energy_j = lax.broadcasted_iota(jnp.int32, (TOTAL, TOTAL), 0)
    energy_k = lax.broadcasted_iota(jnp.int32, (TOTAL, TOTAL), 1)
    spacing = energy_k - energy_j

    def add(m, sums):
        own, side = sums
        shift = shifts[m]
        up, down = spacing == shift, spacing == -shift
        own = own + (jnp.where(up, weights[0, m], 0.0) + jnp.where(down, weights[1, m], 0.0))
        side = side + (jnp.where(up, weights[2, m], 0.0) + jnp.where(down, weights[3, m], 0.0))
        return own, side

    blank = jnp.zeros((TOTAL, TOTAL), jnp.float32)
    sums = lax.fori_loop(0, shifts.shape[0], add, (blank, blank))
    big = TOTAL * ROWS
    spread = (
        lax.broadcasted_iota(jnp.int32, (big, TOTAL), 0) // ROWS
        == lax.broadcasted_iota(jnp.int32, (big, TOTAL), 1)
    ).astype(jnp.bfloat16)
    same = (
        lax.broadcasted_iota(jnp.int32, (big, big), 0) % ROWS
        == lax.broadcasted_iota(jnp.int32, (big, big), 1) % ROWS
    )
    for kernel, out in zip(sums, (own_ref, side_ref)):
        kernel = kernel.astype(jnp.bfloat16)
        tall = jnp.dot(spread, kernel, preferred_element_type=jnp.float32).astype(jnp.bfloat16)
        wide = lax.dot_general(
            tall, spread, (((1,), (1,)), ((), ())), preferred_element_type=jnp.float32
        )
        out[...] = jnp.where(same, wide, 0.0).astype(jnp.bfloat16)


def mixing_weights(shifts, weights):
    shape = jax.ShapeDtypeStruct((TOTAL * ROWS, TOTAL * ROWS), jnp.bfloat16)
    return pl.pallas_call(
        weights_kernel,
        in_specs=[SMEM_SPEC, SMEM_SPEC],
        out_specs=[VMEM_SPEC] * 2,
        out_shape=[shape, shape],
        compiler_params=params(16),
        cost_estimate=cost(2 * 10**9, 4 * 10**6),
        name="mixing_weights",
    )(shifts, weights)


def find_starts(counts, starts):
    so_far = jnp.int32(0)
    for e in range(counts.shape[0]):
        starts[e] = so_far
        so_far = so_far + counts[e]


def pack_kernel(counts, rows, out, starts):
    find_starts(counts, starts)
    for e in range(rows.shape[0]):
        for s in reversed(range(rows.shape[1])):
            row = starts[e] + jnp.where(s < counts[e], s, 0)
            out[row] = rows[e, s]


def pack(counts, rows):
    tiles = rows.shape[2]
    return pl.pallas_call(
        pack_kernel,
        in_specs=[SMEM_SPEC, VMEM_SPEC],
        out_specs=VMEM_SPEC,
        out_shape=jax.ShapeDtypeStruct((TOTAL,) + tile_shape(tiles), jnp.bfloat16),
        scratch_shapes=[pltpu.SMEM(counts.shape, jnp.int32)],
        compiler_params=params(4),
        cost_estimate=cost(0, 4 * rows.size),
        name="pack",
    )(counts, rows)


def mix_kernel(counts, own_ref, side_ref, here, below, above, out, sigma, starts):
    find_starts(counts, starts)
    tiles = here.shape[1]

    def flat(value):
        return value.reshape(TOTAL * ROWS, LANES)

    centre = jnp.concatenate([flat(here[:, t]) for t in range(tiles)], axis=1)
    near = jnp.concatenate([flat(below[:, t] + above[:, t]) for t in range(tiles)], axis=1)
    total = jnp.dot(own_ref[...], centre, preferred_element_type=jnp.float32)
    total = total + jnp.dot(side_ref[...], near, preferred_element_type=jnp.float32)
    total = total.astype(jnp.bfloat16)
    for t in range(tiles):
        sigma[:TOTAL, t] = total[:, t * LANES : (t + 1) * LANES].reshape(TOTAL, ROWS, LANES)
    sigma[TOTAL] = jnp.zeros(sigma.shape[1:], sigma.dtype)
    for e in range(out.shape[0]):
        for s in range(out.shape[1]):
            row = jnp.where(s < counts[e], starts[e] + s, TOTAL)
            out[e, s] = sigma[row]


def mix(counts, own, side, here, below, above, slots):
    tiles = here.shape[1]
    groups = counts.shape[0]
    return pl.pallas_call(
        mix_kernel,
        in_specs=[SMEM_SPEC] + [VMEM_SPEC] * 5,
        out_specs=VMEM_SPEC,
        out_shape=jax.ShapeDtypeStruct((groups, slots) + tile_shape(tiles), jnp.bfloat16),
        scratch_shapes=[
            pltpu.VMEM((TOTAL + 1,) + here.shape[1:], jnp.bfloat16),
            pltpu.SMEM(counts.shape, jnp.int32),
        ],
        compiler_params=params(16),
        cost_estimate=cost(4 * own.size * tiles * LANES, 6 * here.size),
        name="mix",
    )(counts, own, side, here, below, above)


def scatter_kernel(parts, *refs):
    received, (r_ref, out_hbm, right, result, sems) = refs[: len(parts)], refs[len(parts) :]
    slots, _, n, _ = r_ref.shape
    found = homes(parts, received[0].shape[0])
    copies = []
    for s in range(slots):
        for held, part in zip(found, received):
            for owner, t, tile, half, lane in held:
                value = part[owner, s, t]
                row, column = tile * ROWS, lane * LANES
                first, second = (column, n + column) if half == 0 else (n + column, column)
                right[row : row + ROWS, first : first + LANES] = value
                value = value if half == 0 else -value
                right[n + row : n + row + ROWS, second : second + LANES] = value
        left = jnp.concatenate([r_ref[s, 0], r_ref[s, 1]], axis=1)
        product = jnp.dot(left, right[...], preferred_element_type=jnp.float32)
        product = product.astype(jnp.bfloat16)
        result[s, 0] = product[:, :n]
        result[s, 1] = product[:, n:]
        copy = pltpu.make_async_copy(result.at[s], out_hbm.at[s], sems.at[s])
        copy.start()
        copies.append(copy)
    for copy in copies:
        copy.wait()


def scattered_blocks(retarded, received, parts):
    slots, _, n, _ = retarded.shape
    return pl.pallas_call(
        functools.partial(scatter_kernel, parts),
        in_specs=[VMEM_SPEC] * (len(parts) + 1),
        out_specs=HBM_SPEC,
        out_shape=jax.ShapeDtypeStruct(retarded.shape, jnp.bfloat16),
        scratch_shapes=[
            pltpu.VMEM((2 * n, 2 * n), jnp.bfloat16),
            pltpu.VMEM(retarded.shape, jnp.bfloat16),
            pltpu.SemaphoreType.DMA((slots,)),
        ],
        compiler_params=params(32),
        cost_estimate=cost(slots * 8 * n**3, slots * 12 * n * n),
        name="scattered",
    )(*received, retarded)


def on_device(
    retarded_green_blocks, contact_lesser_sigma, energy_counts, phonon_shift, phonon_weight
):
    groups, blocks = lax.axis_size("energy"), lax.axis_size("atoms")
    slots = retarded_green_blocks.shape[1]
    up = [(i, i + 1) for i in range(blocks - 1)]
    down = [(j, i) for i, j in up]
    retarded = retarded_green_blocks[0]
    found = homes(PARTS, groups)
    own, side = mixing_weights(phonon_shift, phonon_weight)
    returned = []
    for held in found:
        lesser = lesser_blocks(retarded, contact_lesser_sigma[0], groups, held)
        rows = lax.all_to_all(lesser, "energy", 0, 0, tiled=True)
        here = pack(energy_counts, rows)
        below = lax.ppermute(here, "atoms", up)
        above = lax.ppermute(here, "atoms", down)
        sigma = mix(energy_counts, own, side, here, below, above, slots)
        returned.append(lax.all_to_all(sigma, "energy", 0, 0, tiled=True))
    return scattered_blocks(retarded, returned, PARTS)[None]


def solution(mesh):
    in_specs = (
        P("atoms", "energy", None, None, None),
        P("atoms", "energy", None, None, None),
        P(),
        P(),
        P(),
    )
    out_specs = P("atoms", "energy", None, None, None)
    return jax.shard_map(
        on_device, mesh=mesh, in_specs=in_specs, out_specs=out_specs, check_vma=False
    )
```
